32 devices in a mesh: dp: 2 (over x), ctx: 4 (over y, core), tensor: 4 (over z).
Axes of the slice: x: 2, y: 2, z: 4, core: 2. Of those that a mesh axis runs over, the one named last changes fastest.
Arguments:
- tokens: bfloat16 [32, 1024, 1024], P('dp', 'ctx'), may hold values from -6 to 6
- segment_ids: int32 [32, 1024], P('dp', 'ctx'), may hold values from 0 to 3, as said below
- norm1_gain: bfloat16 [1024], P(('dp', 'ctx')), may hold values from 0.5 to 1.5
- norm1_shift: bfloat16 [1024], P(('dp', 'ctx')), may hold values from -1.75 to 1.75
- w_query: bfloat16 [1024, 1024], P(('dp', 'ctx'), 'tensor'), may hold values from -0.1875 to 0.1875
- w_key: bfloat16 [1024, 1024], P(('dp', 'ctx'), 'tensor'), may hold values from -0.1875 to 0.1875
- w_value: bfloat16 [1024, 1024], P(('dp', 'ctx'), 'tensor'), may hold values from -0.1875 to 0.1875
- query_bias: bfloat16 [16, 64], P('tensor', ('dp', 'ctx')), may hold values from -1.75 to 1.75
- value_bias: bfloat16 [16, 64], P('tensor', ('dp', 'ctx')), may hold values from -1.75 to 1.75
- w_out: bfloat16 [1024, 1024], P('tensor', ('dp', 'ctx')), may hold values from -0.75 to 0.75
- out_bias: bfloat16 [1024], P(('dp', 'ctx')), may hold values from -1.75 to 1.75
- norm2_gain: bfloat16 [1024], P(('dp', 'ctx')), may hold values from 0.5 to 1.5
- norm2_shift: bfloat16 [1024], P(('dp', 'ctx')), may hold values from -1.75 to 1.75
- w_up: bfloat16 [1024, 4096], P(('dp', 'ctx'), 'tensor'), may hold values from -0.1875 to 0.1875
- up_bias: bfloat16 [16, 256], P('tensor', ('dp', 'ctx')), may hold values from -1.75 to 1.75
- w_down: bfloat16 [4096, 1024], P('tensor', ('dp', 'ctx')), may hold values from -0.1875 to 0.1875
- down_bias: bfloat16 [1024], P(('dp', 'ctx')), may hold values from -1.75 to 1.75
- out_grad: bfloat16 [32, 1024, 1024], P('dp', 'ctx'), may hold values from -6 to 6
Outputs:
- outputs: bfloat16 [32, 1024, 1024], P('dp', 'ctx')
- tokens_grad: bfloat16 [32, 1024, 1024], P('dp', 'ctx')
- norm1_gain_grad: float32 [1024], P(('dp', 'ctx'))
- norm1_shift_grad: float32 [1024], P(('dp', 'ctx'))
- w_query_grad: float32 [1024, 1024], P(('dp', 'ctx'), 'tensor')
- w_key_grad: float32 [1024, 1024], P(('dp', 'ctx'), 'tensor')
- w_value_grad: float32 [1024, 1024], P(('dp', 'ctx'), 'tensor')
- query_bias_grad: float32 [16, 64], P('tensor', ('dp', 'ctx'))
- value_bias_grad: float32 [16, 64], P('tensor', ('dp', 'ctx'))
- w_out_grad: float32 [1024, 1024], P('tensor', ('dp', 'ctx'))
- out_bias_grad: float32 [1024], P(('dp', 'ctx'))
- norm2_gain_grad: float32 [1024], P(('dp', 'ctx'))
- norm2_shift_grad: float32 [1024], P(('dp', 'ctx'))
- w_up_grad: float32 [1024, 4096], P(('dp', 'ctx'), 'tensor')
- up_bias_grad: float32 [16, 256], P('tensor', ('dp', 'ctx'))
- w_down_grad: float32 [4096, 1024], P('tensor', ('dp', 'ctx'))
- down_bias_grad: float32 [1024], P(('dp', 'ctx'))
The draws below stay inside these ranges and needn't reach their ends.
Inputs may be any that keep to these rules, and one draw needn't show every extreme that they name: `segment_ids`: ids start at 0 and never fall along a sequence. In each group of 16 sequences one (drawn) is a single document; every other sequence holds exactly four documents of 200 tokens or more each.
All inputs are finite; a program needn't handle non-finite values.
Results may differ from the reference program's by a relative error of at most 0.017.
Values may be sent and summed in bfloat16 or wider, within the bound.
A program may use at most 384 MiB of HBM per device.

```python
import math
import jax
import jax.numpy as jnp
from jax import lax

D = 1024
HEADS = 16
FF = 4096
LENGTH = 1024
DOC_MIN = 200
SEQS_DP = 16
HEAD_DIM = 64
SEQUENCES = 32


def draw_segment_ids(key, part):
    row_keys = jax.random.split(jax.random.fold_in(key, 11), SEQUENCES)

    def boundary(row_key):
        extra = jax.random.randint(row_key, (3,), 0, LENGTH - 4 * DOC_MIN + 1).astype(jnp.int32)
        extra = jnp.sort(extra)
        return (DOC_MIN * jnp.arange(1, 4, dtype=jnp.int32) + extra).astype(jnp.int32)
    cuts = jax.vmap(boundary)(row_keys)
    groups = SEQUENCES // SEQS_DP
    picked = jax.random.randint(jax.random.fold_in(key, 12), (groups,), 0, SEQS_DP)
    row_index = jnp.arange(SEQUENCES)
    single = row_index % SEQS_DP == picked[row_index // SEQS_DP]
    cuts = jnp.where(single[:, None], LENGTH, cuts)
    places = jnp.arange(LENGTH)
    return jnp.sum((places[None, :, None] >= cuts[:, None, :]).astype(jnp.int32), axis=-1).astype(jnp.int32)


def block_scale(stream_key, dims, cuts, low, high):
    level = 1.0
    for dim, parts in cuts:
        draws = jax.random.uniform(jax.random.fold_in(jax.random.fold_in(stream_key, 6), dim), (parts,), jnp.float32, low / len(cuts), high / len(cuts))
        level = level * jnp.repeat(jnp.exp(draws), dims[dim] // parts).reshape((-1,) + (1,) * (len(dims) - 1 - dim))
    return level


def centred(stream_key, dims, scale, bound, cuts=(), kind=jnp.bfloat16):
    drawn = scale * jax.random.normal(stream_key, dims, jnp.float32)
    if cuts:
        drawn = drawn * block_scale(stream_key, dims, cuts, -0.22, 0.18)
    return jnp.clip(drawn, -bound, bound).astype(kind)


def setup_inputs(seed: int = 0) -> dict:
    key_of = jax.random.split(jax.random.key(seed), 19)
    return {
        "tokens": centred(key_of[0], (SEQUENCES, LENGTH, D), 1.0, 6.0, ((0, 2), (1, 4))),
        "segment_ids": draw_segment_ids(jax.random.fold_in(key_of[18], 71), 0),
        "norm1_gain": jnp.clip(1.0 + 0.1 * jax.random.normal(key_of[2], (D,), jnp.float32), 0.5, 1.5).astype(jnp.bfloat16),
        "norm1_shift": centred(key_of[3], (D,), 0.3, 1.75, ((0, 8),)),
        "w_query": centred(key_of[4], (D, D), D ** -0.5, 0.1875, ((0, 8), (1, 4))),
        "w_key": centred(key_of[5], (D, D), D ** -0.5, 0.1875, ((0, 8), (1, 4))),
        "w_value": centred(key_of[6], (D, D), D ** -0.5, 0.1875, ((0, 8), (1, 4))),
        "query_bias": centred(key_of[7], (HEADS, HEAD_DIM), 0.3, 1.75, ((0, 4), (1, 8))),
        "value_bias": centred(key_of[8], (HEADS, HEAD_DIM), 0.3, 1.75, ((0, 4), (1, 8))),
        "w_out": centred(key_of[9], (D, D), (D // 16) ** -0.5, 0.75, ((0, 4), (1, 8))),
        "out_bias": centred(key_of[10], (D,), 0.3, 1.75, ((0, 8),)),
        "norm2_gain": jnp.clip(1.0 + 0.1 * jax.random.normal(key_of[11], (D,), jnp.float32), 0.5, 1.5).astype(jnp.bfloat16),
        "norm2_shift": centred(key_of[12], (D,), 0.3, 1.75, ((0, 8),)),
        "w_up": centred(key_of[13], (D, FF), D ** -0.5, 0.1875, ((0, 8), (1, 4))),
        "up_bias": centred(key_of[14], (HEADS, FF // HEADS), 0.3, 1.75, ((0, 4), (1, 8))),
        "w_down": centred(key_of[15], (FF, D), (FF // 4) ** -0.5, 0.1875, ((0, 4), (1, 8))),
        "down_bias": centred(key_of[16], (D,), 0.3, 1.75, ((0, 8),)),
        "out_grad": centred(key_of[17], (SEQUENCES, LENGTH, D), 1.0, 6.0, ((0, 2), (1, 4))),
    }


@jax.custom_vjp
def low(v):
    return lax.optimization_barrier(v.astype(jnp.bfloat16)).astype(jnp.float32)

@jax.custom_vjp
def low_back(v):
    return v

def low_keep(v):
    return (low(v), None)

def low_pass(kept, grad):
    return (grad,)

def back_keep(v):
    return (v, None)

def back_low(kept, grad):
    return (low(grad),)
low.defvjp(low_keep, low_pass)
low_back.defvjp(back_keep, back_low)
EPSILON = 1e-05
PRECISION = lax.Precision.HIGHEST

def layer_norm(values, gain, shift):
    centre = values - lax.optimization_barrier(jnp.mean(values, axis=-1, keepdims=True))
    spread = lax.optimization_barrier(jnp.mean(centre * centre, axis=-1, keepdims=True))
    return centre * lax.rsqrt(spread + EPSILON) * gain + shift

def gelu_tanh(values):
    return 0.5 * values * (1.0 + jnp.tanh(0.7978845608028654 * (values + 0.044715 * values * values * values)))

def linear(left, right):
    return jnp.dot(left, right, precision=PRECISION, preferred_element_type=jnp.float32)

def sequence_forward(params, inputs, segment):
    norm1_gain, norm1_shift, w_query, w_key, w_value, query_bias, value_bias, w_out, out_bias, norm2_gain, norm2_shift, w_up, up_bias, w_down, down_bias = params
    normed_one = low(layer_norm(inputs, norm1_gain, norm1_shift))
    queries = low(low_back(linear(normed_one, w_query) + query_bias.reshape(-1)))
    key_rows = low(low_back(linear(normed_one, w_key)))
    value_rows = low(low_back(linear(normed_one, w_value) + value_bias.reshape(-1)))
    query_heads = queries.reshape(LENGTH, HEADS, HEAD_DIM)
    key_heads = key_rows.reshape(LENGTH, HEADS, HEAD_DIM)
    value_heads = value_rows.reshape(LENGTH, HEADS, HEAD_DIM)
    raw_scores = jnp.einsum('qhd,khd->hqk', query_heads, key_heads, precision=PRECISION)
    places = jnp.arange(LENGTH)
    offsets = (places[None, :] - places[:, None]).astype(jnp.float32)
    slopes = jnp.exp2(-8.0 * jnp.arange(1, HEADS + 1).astype(jnp.float32) / HEADS)
    scores = raw_scores * (1.0 / math.sqrt(HEAD_DIM)) + slopes[:, None, None] * offsets[None]
    allowed = (places[None, :] <= places[:, None]) & (segment[None, :] == segment[:, None])
    scores = low_back(jnp.where(allowed[None], scores, -1e+30))
    highest = lax.optimization_barrier(jnp.max(scores, axis=-1, keepdims=True))
    exponent = jnp.exp(scores - highest)
    softmaxed = exponent / lax.optimization_barrier(jnp.sum(exponent, axis=-1, keepdims=True))
    mixed_heads = jnp.einsum('hqk,khd->qhd', low(softmaxed), value_heads, precision=PRECISION).reshape(LENGTH, D)
    mixed_heads = low(low_back(mixed_heads))
    residual = inputs + low_back(linear(mixed_heads, w_out)) + out_bias
    normed_two = low(layer_norm(residual, norm2_gain, norm2_shift))
    activated = low(gelu_tanh(low_back(linear(normed_two, w_up) + up_bias.reshape(-1))))
    return residual + linear(activated, w_down) + down_bias

def reference(tokens, segment_ids, norm1_gain, norm1_shift, w_query, w_key, w_value, query_bias, value_bias, w_out, out_bias, norm2_gain, norm2_shift, w_up, up_bias, w_down, down_bias, out_grad):
    params = (norm1_gain.astype(jnp.float32), norm1_shift.astype(jnp.float32), w_query.astype(jnp.float32), w_key.astype(jnp.float32), w_value.astype(jnp.float32), query_bias.astype(jnp.float32), value_bias.astype(jnp.float32), w_out.astype(jnp.float32), out_bias.astype(jnp.float32), norm2_gain.astype(jnp.float32), norm2_shift.astype(jnp.float32), w_up.astype(jnp.float32), up_bias.astype(jnp.float32), w_down.astype(jnp.float32), down_bias.astype(jnp.float32))
    inputs = tokens.astype(jnp.float32)
    stepper = jax.checkpoint(sequence_forward)

    def forward_all(weights, values):

        def advance(carried, sequence):
            return (carried, stepper(weights, sequence[0], sequence[1]))
        unused, results = lax.scan(advance, jnp.zeros((), jnp.float32), (values, segment_ids))
        return results
    results, pullback = jax.vjp(forward_all, params, inputs)
    param_grads, input_grad = pullback(out_grad.astype(jnp.float32))
    return (results.astype(jnp.bfloat16), input_grad.astype(jnp.bfloat16), param_grads[0], param_grads[1], param_grads[2], param_grads[3], param_grads[4], param_grads[5], param_grads[6], param_grads[7], param_grads[8], param_grads[9], param_grads[10], param_grads[11], param_grads[12], param_grads[13], param_grads[14])
```

```python
import functools
import math

import jax
import jax.numpy as jnp
from jax import lax
from jax.experimental import pallas as pl
from jax.experimental.pallas import tpu as pltpu
from jax.sharding import PartitionSpec as P

HEADS = 16
MICRO = 2
HEAD_DIM = 64


EPSILON = 1e-05


def layer_norm(values, gain, shift):
    centre = values - jnp.mean(values, axis=-1, keepdims=True)
    spread = jnp.mean(centre * centre, axis=-1, keepdims=True)
    return centre * lax.rsqrt(spread + EPSILON) * gain + shift


def gelu_tanh(values):
    return (
        0.5
        * values
        * (1.0 + jnp.tanh(0.7978845608028654 * (values + 0.044715 * values * values * values)))
    )


def matmul(left, right):
    return jnp.dot(left, right, preferred_element_type=jnp.float32)


def matmul_left(left, right):
    return lax.dot_general(
        left, right, (((0,), (0,)), ((), ())), preferred_element_type=jnp.float32
    )


def matmul_right(left, right):
    return lax.dot_general(
        left, right, (((1,), (1,)), ((), ())), preferred_element_type=jnp.float32
    )


def full_total(partial_value):
    return lax.psum(partial_value, "tensor")


def scores_of(query_heads, key_heads, query_seg, key_seg, slopes, query_first):
    query_count = query_heads.shape[1]
    key_count = key_heads.shape[1]
    head_width = query_heads.shape[3]
    raw_scores = jnp.einsum(
        "bqhd,bkhd->bhqk", query_heads, key_heads, preferred_element_type=jnp.float32
    )
    query_place = query_first + jnp.arange(query_count)
    key_place = jnp.arange(key_count)
    offsets = (key_place[None, :] - query_place[:, None]).astype(jnp.float32)
    scores = (
        raw_scores * (1.0 / math.sqrt(head_width))
        + slopes[None, :, None, None] * offsets[None, None]
    )
    causal = (key_place[None, :] <= query_place[:, None])[None, None]
    same_doc = query_seg[:, None, :, None] == key_seg[:, None, None, :]
    return jnp.where(causal & same_doc, scores, -1e30)


def shards(
    tokens,
    segment_ids,
    norm1_gain,
    norm1_shift,
    w_query,
    w_key,
    w_value,
    query_bias,
    value_bias,
    w_out,
    out_bias,
    norm2_gain,
    norm2_shift,
    w_up,
    up_bias,
    w_down,
    down_bias,
    out_grad,
):
    seqs_local, span_len, model_width = tokens.shape
    micro_seqs = seqs_local // MICRO
    row_count = micro_seqs * span_len
    heads_local = query_bias.shape[0]
    cols_local = heads_local * HEAD_DIM
    ff_local = w_up.shape[1]
    length_all = span_len * lax.axis_size("ctx")
    span_first = lax.axis_index("ctx") * span_len
    head_global = lax.axis_index("tensor") * heads_local + jnp.arange(heads_local)
    slopes = jnp.exp2(-8.0 * (head_global + 1).astype(jnp.float32) / HEADS)
    scale = 1.0 / math.sqrt(HEAD_DIM)
    grad_query = jnp.zeros((model_width, cols_local), jnp.float32)
    grad_key = jnp.zeros((model_width, cols_local), jnp.float32)
    grad_value = jnp.zeros((model_width, cols_local), jnp.float32)
    grad_qbias = jnp.zeros((heads_local, HEAD_DIM), jnp.float32)
    grad_vbias = jnp.zeros((heads_local, HEAD_DIM), jnp.float32)
    grad_wout = jnp.zeros((cols_local, model_width), jnp.float32)
    grad_small = jnp.zeros((6, model_width), jnp.float32)
    grad_up = jnp.zeros((model_width, ff_local), jnp.float32)
    grad_ubias = jnp.zeros((heads_local, ff_local // heads_local), jnp.float32)
    grad_down = jnp.zeros((ff_local, model_width), jnp.float32)
    outputs_list = []
    inputs_grad_list = []
    for micro_index in range(MICRO):
        first = micro_index * micro_seqs
        inputs = (
            tokens[first : first + micro_seqs].reshape(row_count, model_width).astype(jnp.float32)
        )
        query_seg = segment_ids[first : first + micro_seqs]
        cotangent = out_grad[first : first + micro_seqs].reshape(row_count, model_width)
        weights = (
            lax.all_gather(norm1_gain, ("dp", "ctx"), axis=0, tiled=True),
            lax.all_gather(norm1_shift, ("dp", "ctx"), axis=0, tiled=True),
            lax.all_gather(w_query, ("dp", "ctx"), axis=0, tiled=True),
            lax.all_gather(w_key, ("dp", "ctx"), axis=0, tiled=True),
            lax.all_gather(w_value, ("dp", "ctx"), axis=0, tiled=True),
            lax.all_gather(query_bias, ("dp", "ctx"), axis=1, tiled=True),
            lax.all_gather(value_bias, ("dp", "ctx"), axis=1, tiled=True),
            lax.all_gather(w_out, ("dp", "ctx"), axis=1, tiled=True),
            lax.all_gather(out_bias, ("dp", "ctx"), axis=0, tiled=True),
            lax.all_gather(norm2_gain, ("dp", "ctx"), axis=0, tiled=True),
            lax.all_gather(norm2_shift, ("dp", "ctx"), axis=0, tiled=True),
            lax.all_gather(w_up, ("dp", "ctx"), axis=0, tiled=True),
            lax.all_gather(up_bias, ("dp", "ctx"), axis=1, tiled=True),
            lax.all_gather(w_down, ("dp", "ctx"), axis=1, tiled=True),
            lax.all_gather(down_bias, ("dp", "ctx"), axis=0, tiled=True),
        )
        (
            gain_one,
            shift_one,
            full_query,
            full_key,
            full_value,
            bias_query,
            bias_value,
            full_out,
            bias_out,
            gain_two,
            shift_two,
            full_up,
            bias_up,
            full_down,
            bias_down,
        ) = weights
        gain_one = gain_one.astype(jnp.float32)
        shift_one = shift_one.astype(jnp.float32)
        gain_two = gain_two.astype(jnp.float32)
        shift_two = shift_two.astype(jnp.float32)
        bias_out = bias_out.astype(jnp.float32)
        bias_down = bias_down.astype(jnp.float32)
        normed_one = layer_norm(inputs, gain_one, shift_one).astype(jnp.bfloat16)
        queries = (
            matmul(normed_one, full_query) + bias_query.reshape(-1).astype(jnp.float32)
        ).astype(jnp.bfloat16)
        key_rows = matmul(normed_one, full_key).astype(jnp.bfloat16)
        value_rows = (
            matmul(normed_one, full_value) + bias_value.reshape(-1).astype(jnp.float32)
        ).astype(jnp.bfloat16)
        local_pairs = jnp.concatenate([key_rows, value_rows], axis=1).reshape(
            micro_seqs, span_len, 2 * cols_local
        )
        pairs_all, key_seg = (
            lax.all_gather(local_pairs, "ctx", axis=1, tiled=True),
            lax.all_gather(query_seg.astype(jnp.bfloat16), "ctx", axis=1, tiled=True),
        )
        key_seg = key_seg.astype(jnp.float32)
        query_segf = query_seg.astype(jnp.float32)
        key_heads = pairs_all[:, :, :cols_local].reshape(
            micro_seqs, length_all, heads_local, HEAD_DIM
        )
        value_heads = pairs_all[:, :, cols_local:].reshape(
            micro_seqs, length_all, heads_local, HEAD_DIM
        )
        query_heads = queries.reshape(micro_seqs, span_len, heads_local, HEAD_DIM)
        scores = scores_of(query_heads, key_heads, query_segf, key_seg, slopes, span_first)
        highest = jnp.max(scores, axis=-1, keepdims=True)
        exponent = jnp.exp(scores - highest)
        totals = jnp.sum(exponent, axis=-1, keepdims=True)
        softmaxed = exponent / totals
        log_total = highest + jnp.log(totals)
        mixed_heads = jnp.einsum(
            "bhqk,bkhd->bqhd",
            softmaxed.astype(jnp.bfloat16),
            value_heads,
            preferred_element_type=jnp.float32,
        )
        mixed_low = mixed_heads.reshape(row_count, cols_local).astype(jnp.bfloat16)
        attn_part = matmul(mixed_low, full_out)
        residual = inputs + full_total(attn_part) + bias_out
        normed_two = layer_norm(residual, gain_two, shift_two).astype(jnp.bfloat16)
        pre_act = matmul(normed_two, full_up) + bias_up.reshape(-1).astype(jnp.float32)
        activated = gelu_tanh(pre_act).astype(jnp.bfloat16)
        mlp_part = matmul(activated, full_down)
        result_rows = (residual + full_total(mlp_part) + bias_down).astype(jnp.bfloat16)
        outputs_list.append(result_rows.reshape(micro_seqs, span_len, model_width))
        weights_back = (
            lax.all_gather(norm1_gain, ("dp", "ctx"), axis=0, tiled=True),
            lax.all_gather(norm1_shift, ("dp", "ctx"), axis=0, tiled=True),
            lax.all_gather(w_query, ("dp", "ctx"), axis=0, tiled=True),
            lax.all_gather(w_key, ("dp", "ctx"), axis=0, tiled=True),
            lax.all_gather(w_value, ("dp", "ctx"), axis=0, tiled=True),
            lax.all_gather(query_bias, ("dp", "ctx"), axis=1, tiled=True),
            lax.all_gather(value_bias, ("dp", "ctx"), axis=1, tiled=True),
            lax.all_gather(w_out, ("dp", "ctx"), axis=1, tiled=True),
            lax.all_gather(out_bias, ("dp", "ctx"), axis=0, tiled=True),
            lax.all_gather(norm2_gain, ("dp", "ctx"), axis=0, tiled=True),
            lax.all_gather(norm2_shift, ("dp", "ctx"), axis=0, tiled=True),
            lax.all_gather(w_up, ("dp", "ctx"), axis=0, tiled=True),
            lax.all_gather(up_bias, ("dp", "ctx"), axis=1, tiled=True),
            lax.all_gather(w_down, ("dp", "ctx"), axis=1, tiled=True),
            lax.all_gather(down_bias, ("dp", "ctx"), axis=0, tiled=True),
        )
        back_query = weights_back[2]
        back_key = weights_back[3]
        back_value = weights_back[4]
        back_out = weights_back[7]
        back_up = weights_back[11]
        back_down = weights_back[13]
        gain_one = weights_back[0].astype(jnp.float32)
        shift_one = weights_back[1].astype(jnp.float32)
        gain_two = weights_back[9].astype(jnp.float32)
        shift_two = weights_back[10].astype(jnp.float32)
        act_grad = matmul_right(cotangent, back_down)
        unused, gelu_pull = jax.vjp(gelu_tanh, pre_act)
        pre_grad = gelu_pull(act_grad)[0].astype(jnp.bfloat16)
        grad_down = grad_down + matmul_left(activated, cotangent)
        grad_ubias = grad_ubias + jnp.sum(pre_grad.astype(jnp.float32), axis=0).reshape(
            heads_local, -1
        )
        grad_up = grad_up + matmul_left(normed_two, pre_grad)
        normed_two_back = matmul_right(pre_grad, back_up)
        unused, norm_pull = jax.vjp(layer_norm, residual, gain_two, shift_two)
        resid_grad, gain_two_grad, shift_two_grad = norm_pull(full_total(normed_two_back))
        cot_rows = cotangent.astype(jnp.float32)
        resid_grad = resid_grad + cot_rows
        attn_grad = resid_grad.astype(jnp.bfloat16)
        grad_wout = grad_wout + matmul_left(mixed_low, attn_grad)
        mixed_grad = matmul_right(attn_grad, back_out).astype(jnp.bfloat16)
        mixed_grad_heads = mixed_grad.reshape(micro_seqs, span_len, heads_local, HEAD_DIM)
        scores = scores_of(query_heads, key_heads, query_segf, key_seg, slopes, span_first)
        softmaxed = jnp.exp(scores - log_total)
        prob_grad = jnp.einsum(
            "bqhd,bkhd->bhqk", mixed_grad_heads, value_heads, preferred_element_type=jnp.float32
        )
        delta = jnp.sum(softmaxed * prob_grad, axis=-1, keepdims=True)
        score_grad = (softmaxed * (prob_grad - delta)).astype(jnp.bfloat16)
        query_grad = (
            jnp.einsum("bhqk,bkhd->bqhd", score_grad, key_heads, preferred_element_type=jnp.float32)
            * scale
        )
        query_low = query_grad.reshape(row_count, cols_local).astype(jnp.bfloat16)
        key_grad = (
            jnp.einsum(
                "bhqk,bqhd->bkhd", score_grad, query_heads, preferred_element_type=jnp.float32
            )
            * scale
        )
        value_grad = jnp.einsum(
            "bhqk,bqhd->bkhd",
            softmaxed.astype(jnp.bfloat16),
            mixed_grad_heads,
            preferred_element_type=jnp.float32,
        )
        pair_grad = jnp.concatenate(
            [
                key_grad.reshape(micro_seqs, length_all, cols_local),
                value_grad.reshape(micro_seqs, length_all, cols_local),
            ],
            axis=2,
        )
        pair_own = lax.psum_scatter(
            pair_grad.astype(jnp.bfloat16), "ctx", scatter_dimension=1, tiled=True
        ).astype(jnp.float32)
        key_low = pair_own[:, :, :cols_local].reshape(row_count, cols_local).astype(jnp.bfloat16)
        value_low = pair_own[:, :, cols_local:].reshape(row_count, cols_local).astype(jnp.bfloat16)
        grad_query = grad_query + matmul_left(normed_one, query_low)
        grad_key = grad_key + matmul_left(normed_one, key_low)
        grad_value = grad_value + matmul_left(normed_one, value_low)
        grad_qbias = grad_qbias + jnp.sum(query_low.astype(jnp.float32), axis=0).reshape(
            heads_local, HEAD_DIM
        )
        grad_vbias = grad_vbias + jnp.sum(value_low.astype(jnp.float32), axis=0).reshape(
            heads_local, HEAD_DIM
        )
        normed_one_back = (
            matmul_right(query_low, back_query)
            + matmul_right(key_low, back_key)
            + matmul_right(value_low, back_value)
        )
        unused, first_pull = jax.vjp(layer_norm, inputs, gain_one, shift_one)
        input_grad, gain_one_grad, shift_one_grad = first_pull(full_total(normed_one_back))
        input_grad = (input_grad + resid_grad).astype(jnp.bfloat16)
        inputs_grad_list.append(input_grad.reshape(micro_seqs, span_len, model_width))
        grad_small = grad_small + jnp.stack(
            [
                gain_one_grad,
                shift_one_grad,
                jnp.sum(resid_grad, axis=0),
                gain_two_grad,
                shift_two_grad,
                jnp.sum(cot_rows, axis=0),
            ],
            axis=0,
        )
    summed = (
        lax.psum_scatter(
            grad_query.astype(jnp.bfloat16), ("dp", "ctx"), scatter_dimension=0, tiled=True
        ).astype(jnp.float32),
        lax.psum_scatter(
            grad_key.astype(jnp.bfloat16), ("dp", "ctx"), scatter_dimension=0, tiled=True
        ).astype(jnp.float32),
        lax.psum_scatter(
            grad_value.astype(jnp.bfloat16), ("dp", "ctx"), scatter_dimension=0, tiled=True
        ).astype(jnp.float32),
        lax.psum_scatter(
            grad_qbias.astype(jnp.bfloat16), ("dp", "ctx"), scatter_dimension=1, tiled=True
        ).astype(jnp.float32),
        lax.psum_scatter(
            grad_vbias.astype(jnp.bfloat16), ("dp", "ctx"), scatter_dimension=1, tiled=True
        ).astype(jnp.float32),
        lax.psum_scatter(
            grad_wout.astype(jnp.bfloat16), ("dp", "ctx"), scatter_dimension=1, tiled=True
        ).astype(jnp.float32),
        lax.psum_scatter(
            grad_small.astype(jnp.bfloat16), ("dp", "ctx"), scatter_dimension=1, tiled=True
        ).astype(jnp.float32),
        lax.psum_scatter(
            grad_up.astype(jnp.bfloat16), ("dp", "ctx"), scatter_dimension=0, tiled=True
        ).astype(jnp.float32),
        lax.psum_scatter(
            grad_ubias.astype(jnp.bfloat16), ("dp", "ctx"), scatter_dimension=1, tiled=True
        ).astype(jnp.float32),
        lax.psum_scatter(
            grad_down.astype(jnp.bfloat16), ("dp", "ctx"), scatter_dimension=1, tiled=True
        ).astype(jnp.float32),
    )
    (
        sum_query,
        sum_key,
        sum_value,
        sum_qbias,
        sum_vbias,
        sum_wout,
        sum_small,
        sum_up,
        sum_ubias,
        sum_down,
    ) = summed
    return (
        jnp.concatenate(outputs_list, axis=0),
        jnp.concatenate(inputs_grad_list, axis=0),
        sum_small[0],
        sum_small[1],
        sum_query,
        sum_key,
        sum_value,
        sum_qbias,
        sum_vbias,
        sum_wout,
        sum_small[2],
        sum_small[3],
        sum_small[4],
        sum_up,
        sum_ubias,
        sum_down,
        sum_small[5],
    )


ALL = ("dp", "ctx", "tensor")
NORMAL = (((1,), (0,)), ((), ()))
ROWS = (((1,), (1,)), ((), ()))
COLS = (((0,), (0,)), ((), ()))
QUERY_BLOCK = 256


def dot(left, right, dims):
    return lax.dot_general(left, right, dims, preferred_element_type=jnp.float32)


def scores_turned(query, key, slope, first, seg_query, seg_key, causal_from):
    count, block = key.shape[0], query.shape[0]
    raw = dot(key, query, ROWS) * (1.0 / math.sqrt(HEAD_DIM))
    key_place = lax.broadcasted_iota(jnp.int32, (count, 1), 0)
    query_place = first + lax.broadcasted_iota(jnp.int32, (1, block), 1)
    scores = raw + slope * (key_place - query_place).astype(jnp.float32)
    allowed = (key_place <= query_place) & (seg_key == seg_query)
    return jnp.where(allowed, scores, -1e30)


def attend_kernel(heads, block, slope_ref, row_ref, col_ref, qkv_ref, o_ref, lse_ref):
    step = pl.program_id(1)
    length = qkv_ref.shape[0]
    width = heads * HEAD_DIM
    for head in range(heads):
        lo = head * HEAD_DIM
        slope = slope_ref[step * heads + head]
        for first in range(0, length, block):
            last = first + block
            query = qkv_ref[first:last, lo : lo + HEAD_DIM]
            key = qkv_ref[0:last, width + lo : width + lo + HEAD_DIM]
            value = qkv_ref[0:last, 2 * width + lo : 2 * width + lo + HEAD_DIM]
            scores = scores_turned(
                query, key, slope, first, row_ref[:, first:last], col_ref[0:last, :], first
            )
            highest = jnp.max(scores, axis=0, keepdims=True)
            exponent = jnp.exp(scores - highest)
            totals = jnp.sum(exponent, axis=0, keepdims=True)
            softmaxed = (exponent * (1.0 / totals)).astype(jnp.bfloat16)
            mixed = dot(softmaxed, value, COLS)
            o_ref[first:last, lo : lo + HEAD_DIM] = mixed.astype(jnp.bfloat16)
            lse_ref[head : head + 1, first:last] = highest + jnp.log(totals)


def attend_back_kernel(
    heads, block, slope_ref, row_ref, col_ref, qkv_ref, do_ref, lse_ref, grad_ref, dk_ref, dv_ref
):
    step = pl.program_id(1)
    length = qkv_ref.shape[0]
    width = heads * HEAD_DIM
    scale = 1.0 / math.sqrt(HEAD_DIM)
    for head in range(heads):
        lo = head * HEAD_DIM
        slope = slope_ref[step * heads + head]
        for first in reversed(range(0, length, block)):
            last = first + block
            query = qkv_ref[first:last, lo : lo + HEAD_DIM]
            key = qkv_ref[0:last, width + lo : width + lo + HEAD_DIM]
            value = qkv_ref[0:last, 2 * width + lo : 2 * width + lo + HEAD_DIM]
            mixed_grad = do_ref[first:last, lo : lo + HEAD_DIM]
            scores = scores_turned(
                query, key, slope, first, row_ref[:, first:last], col_ref[0:last, :], first
            )
            softmaxed = jnp.exp(scores - lse_ref[head : head + 1, first:last])
            prob_grad = dot(value, mixed_grad, ROWS)
            delta = jnp.sum(softmaxed * prob_grad, axis=0, keepdims=True)
            score_grad = (softmaxed * (prob_grad - delta)).astype(jnp.bfloat16)
            prob_low = softmaxed.astype(jnp.bfloat16)
            query_grad = dot(score_grad, key, COLS) * scale
            grad_ref[first:last, lo : lo + HEAD_DIM] = query_grad.astype(jnp.bfloat16)
            key_grad = dot(score_grad, query, NORMAL)
            value_grad = dot(prob_low, mixed_grad, NORMAL)
            if last == length:
                dk_ref[...] = key_grad
                dv_ref[...] = value_grad
            else:
                dk_ref[0:last, :] += key_grad
                dv_ref[0:last, :] += value_grad
        grad_ref[:, width + lo : width + lo + HEAD_DIM] = (dk_ref[...] * scale).astype(jnp.bfloat16)
        grad_ref[:, 2 * width + lo : 2 * width + lo + HEAD_DIM] = dv_ref[...].astype(jnp.bfloat16)


def attention_specs(seqs, length, groups, heads):
    width = heads * HEAD_DIM
    return (
        pl.BlockSpec(memory_space=pltpu.SMEM),
        pl.BlockSpec((None, 1, length), lambda s, t: (s, 0, 0)),
        pl.BlockSpec((None, length, 1), lambda s, t: (s, 0, 0)),
        pl.BlockSpec((None, length, 3 * width), lambda s, t: (s, 0, t)),
        pl.BlockSpec((None, length, width), lambda s, t: (s, 0, t)),
        pl.BlockSpec((None, None, heads, length), lambda s, t: (s, t, 0, 0)),
    )


def attend(slopes, seg_row, seg_col, qkv, groups, heads):
    seqs, length, _ = qkv.shape
    specs = attention_specs(seqs, length, groups, heads)
    block = math.gcd(length, QUERY_BLOCK)
    return pl.pallas_call(
        functools.partial(attend_kernel, heads, block),
        grid=(seqs, groups),
        in_specs=list(specs[:4]),
        out_specs=[specs[4], specs[5]],
        out_shape=[
            jax.ShapeDtypeStruct((seqs, length, groups * heads * HEAD_DIM), jnp.bfloat16),
            jax.ShapeDtypeStruct((seqs, groups, heads, length), jnp.float32),
        ],
        compiler_params=pltpu.CompilerParams(vmem_limit_bytes=40 * 2**20),
        name="attend",
    )(slopes, seg_row, seg_col, qkv)


def attend_back(slopes, seg_row, seg_col, qkv, mixed_grad, log_total, groups, heads):
    seqs, length, _ = qkv.shape
    specs = attention_specs(seqs, length, groups, heads)
    block = math.gcd(length, QUERY_BLOCK)
    return pl.pallas_call(
        functools.partial(attend_back_kernel, heads, block),
        grid=(seqs, groups),
        in_specs=list(specs),
        out_specs=specs[3],
        out_shape=jax.ShapeDtypeStruct(qkv.shape, jnp.bfloat16),
        scratch_shapes=[
            pltpu.VMEM((length, HEAD_DIM), jnp.float32),
            pltpu.VMEM((length, HEAD_DIM), jnp.float32),
        ],
        compiler_params=pltpu.CompilerParams(vmem_limit_bytes=40 * 2**20),
        name="attend_back",
    )(slopes, seg_row, seg_col, qkv, mixed_grad, log_total)


def whole_sequences(
    tokens,
    segment_ids,
    norm1_gain,
    norm1_shift,
    w_query,
    w_key,
    w_value,
    query_bias,
    value_bias,
    w_out,
    out_bias,
    norm2_gain,
    norm2_shift,
    w_up,
    up_bias,
    w_down,
    down_bias,
    out_grad,
):
    dps, ctxs, groups = (lax.axis_size(name) for name in ALL)
    owners = dps * ctxs
    place = lax.axis_index("tensor")
    seqs_local, span, model = tokens.shape
    per_group = seqs_local // groups
    seqs = per_group // ctxs
    length = span * ctxs
    rows = seqs * length
    heads = query_bias.shape[0]
    width = heads * HEAD_DIM
    shard = w_query.shape[0]
    hidden = w_up.shape[1]
    shared = query_bias.shape[1]
    shared_up = up_bias.shape[1]

    def gather(value):
        whole = lax.all_gather(value, ALL, axis=0, tiled=False)
        return whole.reshape((owners, groups) + value.shape)

    def to_sequences(value):
        mine = lax.dynamic_slice_in_dim(value, place * per_group, per_group, axis=0)
        return lax.all_to_all(mine, "ctx", split_axis=0, concat_axis=1, tiled=True)

    def to_spans(value):
        mine = lax.all_to_all(value, "ctx", split_axis=1, concat_axis=0, tiled=True)
        return lax.all_gather(mine, "tensor", axis=0, tiled=True)

    def scatter(value):
        return lax.psum_scatter(value, ALL, scatter_dimension=0, tiled=True)

    small = jnp.concatenate(
        [
            norm1_gain,
            norm1_shift,
            out_bias,
            norm2_gain,
            norm2_shift,
            down_bias,
            query_bias.reshape(-1),
            value_bias.reshape(-1),
            up_bias.reshape(-1),
        ]
    )
    small = gather(small)
    vectors = small[:, 0, : 6 * shard].reshape(owners, 6, shard).transpose(1, 0, 2)
    vectors = vectors.reshape(6, model).astype(jnp.float32)
    gain_one, shift_one, bias_out, gain_two, shift_two, bias_down = (
        vectors[index] for index in range(6)
    )

    def heads_bias(first, columns):
        part = small[:, :, first : first + heads * columns]
        part = part.reshape(owners, groups, heads, columns).transpose(1, 2, 0, 3)
        return part.reshape(groups, heads * columns * owners).astype(jnp.float32)

    bias_first = 6 * shard
    bias_query = heads_bias(bias_first, shared)
    bias_value = heads_bias(bias_first + heads * shared, shared)
    bias_up = heads_bias(bias_first + 2 * heads * shared, shared_up).reshape(-1)
    bias_qkv = jnp.stack([bias_query, jnp.zeros_like(bias_query), bias_value], axis=1).reshape(-1)

    full_qkv = gather(jnp.concatenate([w_query, w_key, w_value], axis=1))
    full_qkv = full_qkv.transpose(0, 2, 1, 3).reshape(model, groups * 3 * width)
    full_out = gather(w_out).transpose(1, 2, 0, 3).reshape(groups * width, model)
    full_up = gather(w_up).transpose(0, 2, 1, 3).reshape(model, groups * hidden)
    full_down = gather(w_down).transpose(1, 2, 0, 3).reshape(groups * hidden, model)

    inputs_low = to_sequences(tokens)
    segs = to_sequences(segment_ids)
    cotangent = to_sequences(out_grad).reshape(rows, model)
    seg_row = segs.reshape(seqs, 1, length)
    seg_col = segs.reshape(seqs, length, 1)
    slopes = jnp.exp2(-8.0 * jnp.arange(1, HEADS + 1).astype(jnp.float32) / HEADS)

    inputs = inputs_low.reshape(rows, model).astype(jnp.float32)
    normed_one = layer_norm(inputs, gain_one, shift_one).astype(jnp.bfloat16)
    qkv = (matmul(normed_one, full_qkv) + bias_qkv).astype(jnp.bfloat16)
    qkv = qkv.reshape(seqs, length, groups * 3 * width)
    mixed, log_total = attend(slopes, seg_row, seg_col, qkv, groups, heads)
    mixed = mixed.reshape(rows, groups * width)
    residual = inputs + matmul(mixed, full_out) + bias_out
    normed_two = layer_norm(residual, gain_two, shift_two).astype(jnp.bfloat16)
    pre_act = matmul(normed_two, full_up) + bias_up
    activated = gelu_tanh(pre_act).astype(jnp.bfloat16)
    result = (residual + matmul(activated, full_down) + bias_down).astype(jnp.bfloat16)
    outputs = to_spans(result.reshape(seqs, length, model))

    act_grad = matmul_right(cotangent, full_down)
    unused, gelu_pull = jax.vjp(gelu_tanh, pre_act)
    pre_grad = gelu_pull(act_grad)[0].astype(jnp.bfloat16)
    grad_down = matmul_left(activated, cotangent)
    grad_down = grad_down.reshape(groups, hidden, owners, shard).transpose(2, 0, 1, 3)
    sum_down = scatter(grad_down.astype(jnp.bfloat16).reshape(-1, shard)).astype(jnp.float32)
    grad_ubias = jnp.sum(pre_grad.astype(jnp.float32), axis=0)
    grad_up = matmul_left(normed_two, pre_grad)
    grad_up = grad_up.reshape(owners, shard, groups, hidden).transpose(0, 2, 1, 3)
    sum_up = scatter(grad_up.astype(jnp.bfloat16).reshape(-1, hidden)).astype(jnp.float32)
    normed_two_back = matmul_right(pre_grad, full_up)
    unused, norm_pull = jax.vjp(layer_norm, residual, gain_two, shift_two)
    resid_grad, gain_two_grad, shift_two_grad = norm_pull(normed_two_back)
    cot_rows = cotangent.astype(jnp.float32)
    resid_grad = resid_grad + cot_rows
    attn_grad = resid_grad.astype(jnp.bfloat16)
    mixed_grad = matmul_right(attn_grad, full_out).astype(jnp.bfloat16)
    grad_wout = matmul_left(mixed, attn_grad)
    grad_wout = grad_wout.reshape(groups, width, owners, shard).transpose(2, 0, 1, 3)
    sum_wout = scatter(grad_wout.astype(jnp.bfloat16).reshape(-1, shard)).astype(jnp.float32)
    qkv_grad = attend_back(
        slopes,
        seg_row,
        seg_col,
        qkv,
        mixed_grad.reshape(seqs, length, groups * width),
        log_total,
        groups,
        heads,
    ).reshape(rows, groups * 3 * width)
    normed_one_back = matmul_right(qkv_grad, full_qkv)
    unused, first_pull = jax.vjp(layer_norm, inputs, gain_one, shift_one)
    input_grad, gain_one_grad, shift_one_grad = first_pull(normed_one_back)
    input_grad = (input_grad + resid_grad).astype(jnp.bfloat16)
    tokens_grad = to_spans(input_grad.reshape(seqs, length, model))
    grad_qkv = matmul_left(normed_one, qkv_grad)
    grad_qkv = grad_qkv.reshape(owners, shard, groups, 3 * width).transpose(0, 2, 1, 3)
    sum_qkv = scatter(grad_qkv.astype(jnp.bfloat16).reshape(-1, 3 * width)).astype(jnp.float32)
    grad_bias = jnp.sum(qkv_grad.astype(jnp.float32), axis=0).reshape(groups, 3, heads, HEAD_DIM)

    grad_vectors = jnp.stack(
        [
            gain_one_grad,
            shift_one_grad,
            jnp.sum(resid_grad, axis=0),
            gain_two_grad,
            shift_two_grad,
            jnp.sum(cot_rows, axis=0),
        ]
    )
    grad_vectors = grad_vectors.reshape(6, owners, shard).transpose(1, 0, 2)
    grad_vectors = jnp.broadcast_to(
        grad_vectors.reshape(owners, 1, 6 * shard), (owners, groups, 6 * shard)
    )

    def owner_bias(value, columns):
        value = value.reshape(groups, heads, owners, columns).transpose(2, 0, 1, 3)
        return value.reshape(owners, groups, heads * columns)

    grad_small = jnp.concatenate(
        [
            grad_vectors,
            owner_bias(grad_bias[:, 0], shared),
            owner_bias(grad_bias[:, 2], shared),
            owner_bias(grad_ubias, shared_up),
        ],
        axis=2,
    )
    sum_small = scatter(grad_small.reshape(owners * groups, -1))[0]
    sums = sum_small[: 6 * shard].reshape(6, shard)
    sum_biases = sum_small[6 * shard :]
    count = heads * shared
    return (
        outputs,
        tokens_grad,
        sums[0],
        sums[1],
        sum_qkv[:, :width],
        sum_qkv[:, width : 2 * width],
        sum_qkv[:, 2 * width :],
        sum_biases[:count].reshape(heads, shared),
        sum_biases[count : 2 * count].reshape(heads, shared),
        sum_wout,
        sums[2],
        sums[3],
        sums[4],
        sum_up,
        sum_biases[2 * count :].reshape(heads, shared_up),
        sum_down,
        sums[5],
    )


def choose_plan(tokens, *others):
    if tokens.shape[0] % (lax.axis_size("ctx") * lax.axis_size("tensor")) == 0:
        return whole_sequences(tokens, *others)
    return shards(tokens, *others)


def solution(mesh):
    return jax.shard_map(
        choose_plan,
        mesh=mesh,
        in_specs=(
            P("dp", "ctx", None),
            P("dp", "ctx"),
            P(("dp", "ctx")),
            P(("dp", "ctx")),
            P(("dp", "ctx"), "tensor"),
            P(("dp", "ctx"), "tensor"),
            P(("dp", "ctx"), "tensor"),
            P("tensor", ("dp", "ctx")),
            P("tensor", ("dp", "ctx")),
            P("tensor", ("dp", "ctx")),
            P(("dp", "ctx")),
            P(("dp", "ctx")),
            P(("dp", "ctx")),
            P(("dp", "ctx"), "tensor"),
            P("tensor", ("dp", "ctx")),
            P("tensor", ("dp", "ctx")),
            P(("dp", "ctx")),
            P("dp", "ctx", None),
        ),
        out_specs=(
            P("dp", "ctx", None),
            P("dp", "ctx", None),
            P(("dp", "ctx")),
            P(("dp", "ctx")),
            P(("dp", "ctx"), "tensor"),
            P(("dp", "ctx"), "tensor"),
            P(("dp", "ctx"), "tensor"),
            P("tensor", ("dp", "ctx")),
            P("tensor", ("dp", "ctx")),
            P("tensor", ("dp", "ctx")),
            P(("dp", "ctx")),
            P(("dp", "ctx")),
            P(("dp", "ctx")),
            P(("dp", "ctx"), "tensor"),
            P("tensor", ("dp", "ctx")),
            P("tensor", ("dp", "ctx")),
            P(("dp", "ctx")),
        ),
        check_vma=False,
    )
```

```python
import functools
import math

import jax
import jax.numpy as jnp
from jax import lax
from jax.experimental import pallas as pl
from jax.experimental.pallas import tpu as pltpu
from jax.sharding import PartitionSpec as P

HEADS = 16
MICRO = 2
HEAD_DIM = 64


EPSILON = 1e-05


def layer_norm(values, gain, shift):
    centre = values - jnp.mean(values, axis=-1, keepdims=True)
    spread = jnp.mean(centre * centre, axis=-1, keepdims=True)
    return centre * lax.rsqrt(spread + EPSILON) * gain + shift


def gelu_tanh(values):
    return (
        0.5
        * values
        * (1.0 + jnp.tanh(0.7978845608028654 * (values + 0.044715 * values * values * values)))
    )


def matmul(left, right):
    return jnp.dot(left, right, preferred_element_type=jnp.float32)


def matmul_left(left, right):
    return lax.dot_general(
        left, right, (((0,), (0,)), ((), ())), preferred_element_type=jnp.float32
    )


def matmul_right(left, right):
    return lax.dot_general(
        left, right, (((1,), (1,)), ((), ())), preferred_element_type=jnp.float32
    )


def full_total(partial_value):
    return lax.psum(partial_value, "tensor")


def scores_of(query_heads, key_heads, query_seg, key_seg, slopes, query_first):
    query_count = query_heads.shape[1]
    key_count = key_heads.shape[1]
    head_width = query_heads.shape[3]
    raw_scores = jnp.einsum(
        "bqhd,bkhd->bhqk", query_heads, key_heads, preferred_element_type=jnp.float32
    )
    query_place = query_first + jnp.arange(query_count)
    key_place = jnp.arange(key_count)
    offsets = (key_place[None, :] - query_place[:, None]).astype(jnp.float32)
    scores = (
        raw_scores * (1.0 / math.sqrt(head_width))
        + slopes[None, :, None, None] * offsets[None, None]
    )
    causal = (key_place[None, :] <= query_place[:, None])[None, None]
    same_doc = query_seg[:, None, :, None] == key_seg[:, None, None, :]
    return jnp.where(causal & same_doc, scores, -1e30)


def shards(
    tokens,
    segment_ids,
    norm1_gain,
    norm1_shift,
    w_query,
    w_key,
    w_value,
    query_bias,
    value_bias,
    w_out,
    out_bias,
    norm2_gain,
    norm2_shift,
    w_up,
    up_bias,
    w_down,
    down_bias,
    out_grad,
):
    seqs_local, span_len, model_width = tokens.shape
    micro_seqs = seqs_local // MICRO
    row_count = micro_seqs * span_len
    heads_local = query_bias.shape[0]
    cols_local = heads_local * HEAD_DIM
    ff_local = w_up.shape[1]
    length_all = span_len * lax.axis_size("ctx")
    span_first = lax.axis_index("ctx") * span_len
    head_global = lax.axis_index("tensor") * heads_local + jnp.arange(heads_local)
    slopes = jnp.exp2(-8.0 * (head_global + 1).astype(jnp.float32) / HEADS)
    scale = 1.0 / math.sqrt(HEAD_DIM)
    grad_query = jnp.zeros((model_width, cols_local), jnp.float32)
    grad_key = jnp.zeros((model_width, cols_local), jnp.float32)
    grad_value = jnp.zeros((model_width, cols_local), jnp.float32)
    grad_qbias = jnp.zeros((heads_local, HEAD_DIM), jnp.float32)
    grad_vbias = jnp.zeros((heads_local, HEAD_DIM), jnp.float32)
    grad_wout = jnp.zeros((cols_local, model_width), jnp.float32)
    grad_small = jnp.zeros((6, model_width), jnp.float32)
    grad_up = jnp.zeros((model_width, ff_local), jnp.float32)
    grad_ubias = jnp.zeros((heads_local, ff_local // heads_local), jnp.float32)
    grad_down = jnp.zeros((ff_local, model_width), jnp.float32)
    outputs_list = []
    inputs_grad_list = []
    for micro_index in range(MICRO):
        first = micro_index * micro_seqs
        inputs = (
            tokens[first : first + micro_seqs].reshape(row_count, model_width).astype(jnp.float32)
        )
        query_seg = segment_ids[first : first + micro_seqs]
        cotangent = out_grad[first : first + micro_seqs].reshape(row_count, model_width)
        weights = (
            lax.all_gather(norm1_gain, ("dp", "ctx"), axis=0, tiled=True),
            lax.all_gather(norm1_shift, ("dp", "ctx"), axis=0, tiled=True),
            lax.all_gather(w_query, ("dp", "ctx"), axis=0, tiled=True),
            lax.all_gather(w_key, ("dp", "ctx"), axis=0, tiled=True),
            lax.all_gather(w_value, ("dp", "ctx"), axis=0, tiled=True),
            lax.all_gather(query_bias, ("dp", "ctx"), axis=1, tiled=True),
            lax.all_gather(value_bias, ("dp", "ctx"), axis=1, tiled=True),
            lax.all_gather(w_out, ("dp", "ctx"), axis=1, tiled=True),
            lax.all_gather(out_bias, ("dp", "ctx"), axis=0, tiled=True),
            lax.all_gather(norm2_gain, ("dp", "ctx"), axis=0, tiled=True),
            lax.all_gather(norm2_shift, ("dp", "ctx"), axis=0, tiled=True),
            lax.all_gather(w_up, ("dp", "ctx"), axis=0, tiled=True),
            lax.all_gather(up_bias, ("dp", "ctx"), axis=1, tiled=True),
            lax.all_gather(w_down, ("dp", "ctx"), axis=1, tiled=True),
            lax.all_gather(down_bias, ("dp", "ctx"), axis=0, tiled=True),
        )
        (
            gain_one,
            shift_one,
            full_query,
            full_key,
            full_value,
            bias_query,
            bias_value,
            full_out,
            bias_out,
            gain_two,
            shift_two,
            full_up,
            bias_up,
            full_down,
            bias_down,
        ) = weights
        gain_one = gain_one.astype(jnp.float32)
        shift_one = shift_one.astype(jnp.float32)
        gain_two = gain_two.astype(jnp.float32)
        shift_two = shift_two.astype(jnp.float32)
        bias_out = bias_out.astype(jnp.float32)
        bias_down = bias_down.astype(jnp.float32)
        normed_one = layer_norm(inputs, gain_one, shift_one).astype(jnp.bfloat16)
        queries = (
            matmul(normed_one, full_query) + bias_query.reshape(-1).astype(jnp.float32)
        ).astype(jnp.bfloat16)
        key_rows = matmul(normed_one, full_key).astype(jnp.bfloat16)
        value_rows = (
            matmul(normed_one, full_value) + bias_value.reshape(-1).astype(jnp.float32)
        ).astype(jnp.bfloat16)
        local_pairs = jnp.concatenate([key_rows, value_rows], axis=1).reshape(
            micro_seqs, span_len, 2 * cols_local
        )
        pairs_all, key_seg = (
            lax.all_gather(local_pairs, "ctx", axis=1, tiled=True),
            lax.all_gather(query_seg.astype(jnp.bfloat16), "ctx", axis=1, tiled=True),
        )
        key_seg = key_seg.astype(jnp.float32)
        query_segf = query_seg.astype(jnp.float32)
        key_heads = pairs_all[:, :, :cols_local].reshape(
            micro_seqs, length_all, heads_local, HEAD_DIM
        )
        value_heads = pairs_all[:, :, cols_local:].reshape(
            micro_seqs, length_all, heads_local, HEAD_DIM
        )
        query_heads = queries.reshape(micro_seqs, span_len, heads_local, HEAD_DIM)
        scores = scores_of(query_heads, key_heads, query_segf, key_seg, slopes, span_first)
        highest = jnp.max(scores, axis=-1, keepdims=True)
        exponent = jnp.exp(scores - highest)
        totals = jnp.sum(exponent, axis=-1, keepdims=True)
        softmaxed = exponent / totals
        log_total = highest + jnp.log(totals)
        mixed_heads = jnp.einsum(
            "bhqk,bkhd->bqhd",
            softmaxed.astype(jnp.bfloat16),
            value_heads,
            preferred_element_type=jnp.float32,
        )
        mixed_low = mixed_heads.reshape(row_count, cols_local).astype(jnp.bfloat16)
        attn_part = matmul(mixed_low, full_out)
        residual = inputs + full_total(attn_part) + bias_out
        normed_two = layer_norm(residual, gain_two, shift_two).astype(jnp.bfloat16)
        pre_act = matmul(normed_two, full_up) + bias_up.reshape(-1).astype(jnp.float32)
        activated = gelu_tanh(pre_act).astype(jnp.bfloat16)
        mlp_part = matmul(activated, full_down)
        result_rows = (residual + full_total(mlp_part) + bias_down).astype(jnp.bfloat16)
        outputs_list.append(result_rows.reshape(micro_seqs, span_len, model_width))
        weights_back = (
            lax.all_gather(norm1_gain, ("dp", "ctx"), axis=0, tiled=True),
            lax.all_gather(norm1_shift, ("dp", "ctx"), axis=0, tiled=True),
            lax.all_gather(w_query, ("dp", "ctx"), axis=0, tiled=True),
            lax.all_gather(w_key, ("dp", "ctx"), axis=0, tiled=True),
            lax.all_gather(w_value, ("dp", "ctx"), axis=0, tiled=True),
            lax.all_gather(query_bias, ("dp", "ctx"), axis=1, tiled=True),
            lax.all_gather(value_bias, ("dp", "ctx"), axis=1, tiled=True),
            lax.all_gather(w_out, ("dp", "ctx"), axis=1, tiled=True),
            lax.all_gather(out_bias, ("dp", "ctx"), axis=0, tiled=True),
            lax.all_gather(norm2_gain, ("dp", "ctx"), axis=0, tiled=True),
            lax.all_gather(norm2_shift, ("dp", "ctx"), axis=0, tiled=True),
            lax.all_gather(w_up, ("dp", "ctx"), axis=0, tiled=True),
            lax.all_gather(up_bias, ("dp", "ctx"), axis=1, tiled=True),
            lax.all_gather(w_down, ("dp", "ctx"), axis=1, tiled=True),
            lax.all_gather(down_bias, ("dp", "ctx"), axis=0, tiled=True),
        )
        back_query = weights_back[2]
        back_key = weights_back[3]
        back_value = weights_back[4]
        back_out = weights_back[7]
        back_up = weights_back[11]
        back_down = weights_back[13]
        gain_one = weights_back[0].astype(jnp.float32)
        shift_one = weights_back[1].astype(jnp.float32)
        gain_two = weights_back[9].astype(jnp.float32)
        shift_two = weights_back[10].astype(jnp.float32)
        act_grad = matmul_right(cotangent, back_down)
        unused, gelu_pull = jax.vjp(gelu_tanh, pre_act)
        pre_grad = gelu_pull(act_grad)[0].astype(jnp.bfloat16)
        grad_down = grad_down + matmul_left(activated, cotangent)
        grad_ubias = grad_ubias + jnp.sum(pre_grad.astype(jnp.float32), axis=0).reshape(
            heads_local, -1
        )
        grad_up = grad_up + matmul_left(normed_two, pre_grad)
        normed_two_back = matmul_right(pre_grad, back_up)
        unused, norm_pull = jax.vjp(layer_norm, residual, gain_two, shift_two)
        resid_grad, gain_two_grad, shift_two_grad = norm_pull(full_total(normed_two_back))
        cot_rows = cotangent.astype(jnp.float32)
        resid_grad = resid_grad + cot_rows
        attn_grad = resid_grad.astype(jnp.bfloat16)
        grad_wout = grad_wout + matmul_left(mixed_low, attn_grad)
        mixed_grad = matmul_right(attn_grad, back_out).astype(jnp.bfloat16)
        mixed_grad_heads = mixed_grad.reshape(micro_seqs, span_len, heads_local, HEAD_DIM)
        scores = scores_of(query_heads, key_heads, query_segf, key_seg, slopes, span_first)
        softmaxed = jnp.exp(scores - log_total)
        prob_grad = jnp.einsum(
            "bqhd,bkhd->bhqk", mixed_grad_heads, value_heads, preferred_element_type=jnp.float32
        )
        delta = jnp.sum(softmaxed * prob_grad, axis=-1, keepdims=True)
        score_grad = (softmaxed * (prob_grad - delta)).astype(jnp.bfloat16)
        query_grad = (
            jnp.einsum("bhqk,bkhd->bqhd", score_grad, key_heads, preferred_element_type=jnp.float32)
            * scale
        )
        query_low = query_grad.reshape(row_count, cols_local).astype(jnp.bfloat16)
        key_grad = (
            jnp.einsum(
                "bhqk,bqhd->bkhd", score_grad, query_heads, preferred_element_type=jnp.float32
            )
            * scale
        )
        value_grad = jnp.einsum(
            "bhqk,bqhd->bkhd",
            softmaxed.astype(jnp.bfloat16),
            mixed_grad_heads,
            preferred_element_type=jnp.float32,
        )
        pair_grad = jnp.concatenate(
            [
                key_grad.reshape(micro_seqs, length_all, cols_local),
                value_grad.reshape(micro_seqs, length_all, cols_local),
            ],
            axis=2,
        )
        pair_own = lax.psum_scatter(
            pair_grad.astype(jnp.bfloat16), "ctx", scatter_dimension=1, tiled=True
        ).astype(jnp.float32)
        key_low = pair_own[:, :, :cols_local].reshape(row_count, cols_local).astype(jnp.bfloat16)
        value_low = pair_own[:, :, cols_local:].reshape(row_count, cols_local).astype(jnp.bfloat16)
        grad_query = grad_query + matmul_left(normed_one, query_low)
        grad_key = grad_key + matmul_left(normed_one, key_low)
        grad_value = grad_value + matmul_left(normed_one, value_low)
        grad_qbias = grad_qbias + jnp.sum(query_low.astype(jnp.float32), axis=0).reshape(
            heads_local, HEAD_DIM
        )
        grad_vbias = grad_vbias + jnp.sum(value_low.astype(jnp.float32), axis=0).reshape(
            heads_local, HEAD_DIM
        )
        normed_one_back = (
            matmul_right(query_low, back_query)
            + matmul_right(key_low, back_key)
            + matmul_right(value_low, back_value)
        )
        unused, first_pull = jax.vjp(layer_norm, inputs, gain_one, shift_one)
        input_grad, gain_one_grad, shift_one_grad = first_pull(full_total(normed_one_back))
        input_grad = (input_grad + resid_grad).astype(jnp.bfloat16)
        inputs_grad_list.append(input_grad.reshape(micro_seqs, span_len, model_width))
        grad_small = grad_small + jnp.stack(
            [
                gain_one_grad,
                shift_one_grad,
                jnp.sum(resid_grad, axis=0),
                gain_two_grad,
                shift_two_grad,
                jnp.sum(cot_rows, axis=0),
            ],
            axis=0,
        )
    summed = (
        lax.psum_scatter(
            grad_query.astype(jnp.bfloat16), ("dp", "ctx"), scatter_dimension=0, tiled=True
        ).astype(jnp.float32),
        lax.psum_scatter(
            grad_key.astype(jnp.bfloat16), ("dp", "ctx"), scatter_dimension=0, tiled=True
        ).astype(jnp.float32),
        lax.psum_scatter(
            grad_value.astype(jnp.bfloat16), ("dp", "ctx"), scatter_dimension=0, tiled=True
        ).astype(jnp.float32),
        lax.psum_scatter(
            grad_qbias.astype(jnp.bfloat16), ("dp", "ctx"), scatter_dimension=1, tiled=True
        ).astype(jnp.float32),
        lax.psum_scatter(
            grad_vbias.astype(jnp.bfloat16), ("dp", "ctx"), scatter_dimension=1, tiled=True
        ).astype(jnp.float32),
        lax.psum_scatter(
            grad_wout.astype(jnp.bfloat16), ("dp", "ctx"), scatter_dimension=1, tiled=True
        ).astype(jnp.float32),
        lax.psum_scatter(
            grad_small.astype(jnp.bfloat16), ("dp", "ctx"), scatter_dimension=1, tiled=True
        ).astype(jnp.float32),
        lax.psum_scatter(
            grad_up.astype(jnp.bfloat16), ("dp", "ctx"), scatter_dimension=0, tiled=True
        ).astype(jnp.float32),
        lax.psum_scatter(
            grad_ubias.astype(jnp.bfloat16), ("dp", "ctx"), scatter_dimension=1, tiled=True
        ).astype(jnp.float32),
        lax.psum_scatter(
            grad_down.astype(jnp.bfloat16), ("dp", "ctx"), scatter_dimension=1, tiled=True
        ).astype(jnp.float32),
    )
    (
        sum_query,
        sum_key,
        sum_value,
        sum_qbias,
        sum_vbias,
        sum_wout,
        sum_small,
        sum_up,
        sum_ubias,
        sum_down,
    ) = summed
    return (
        jnp.concatenate(outputs_list, axis=0),
        jnp.concatenate(inputs_grad_list, axis=0),
        sum_small[0],
        sum_small[1],
        sum_query,
        sum_key,
        sum_value,
        sum_qbias,
        sum_vbias,
        sum_wout,
        sum_small[2],
        sum_small[3],
        sum_small[4],
        sum_up,
        sum_ubias,
        sum_down,
        sum_small[5],
    )


ALL = ("dp", "ctx", "tensor")
NORMAL = (((1,), (0,)), ((), ()))
ROWS = (((1,), (1,)), ((), ()))
COLS = (((0,), (0,)), ((), ()))
QUERY_BLOCK = 256


def dot(left, right, dims):
    return lax.dot_general(left, right, dims, preferred_element_type=jnp.float32)


def scores_turned(query, key, slope, first, seg_query, seg_key, causal_from):
    count, block = key.shape[0], query.shape[0]
    raw = dot(key, query, ROWS) * (1.0 / math.sqrt(HEAD_DIM))
    key_place = lax.broadcasted_iota(jnp.int32, (count, 1), 0)
    query_place = first + lax.broadcasted_iota(jnp.int32, (1, block), 1)
    scores = raw + slope * (key_place - query_place).astype(jnp.float32)
    allowed = (key_place <= query_place) & (seg_key == seg_query)
    return jnp.where(allowed, scores, -1e30)


def attend_kernel(heads, block, slope_ref, row_ref, col_ref, qkv_ref, o_ref, lse_ref):
    step = pl.program_id(1)
    length = qkv_ref.shape[0]
    width = heads * HEAD_DIM
    for head in range(heads):
        lo = head * HEAD_DIM
        slope = slope_ref[step * heads + head]
        for first in range(0, length, block):
            last = first + block
            query = qkv_ref[first:last, lo : lo + HEAD_DIM]
            key = qkv_ref[0:last, width + lo : width + lo + HEAD_DIM]
            value = qkv_ref[0:last, 2 * width + lo : 2 * width + lo + HEAD_DIM]
            scores = scores_turned(
                query, key, slope, first, row_ref[:, first:last], col_ref[0:last, :], first
            )
            highest = jnp.max(scores, axis=0, keepdims=True)
            exponent = jnp.exp(scores - highest)
            totals = jnp.sum(exponent, axis=0, keepdims=True)
            softmaxed = (exponent * (1.0 / totals)).astype(jnp.bfloat16)
            mixed = dot(softmaxed, value, COLS)
            o_ref[first:last, lo : lo + HEAD_DIM] = mixed.astype(jnp.bfloat16)
            lse_ref[head : head + 1, first:last] = highest + jnp.log(totals)


def attend_back_kernel(
    heads, block, slope_ref, row_ref, col_ref, qkv_ref, do_ref, lse_ref, grad_ref, dk_ref, dv_ref
):
    step = pl.program_id(1)
    length = qkv_ref.shape[0]
    width = heads * HEAD_DIM
    scale = 1.0 / math.sqrt(HEAD_DIM)
    for head in range(heads):
        lo = head * HEAD_DIM
        slope = slope_ref[step * heads + head]
        for first in reversed(range(0, length, block)):
            last = first + block
            query = qkv_ref[first:last, lo : lo + HEAD_DIM]
            key = qkv_ref[0:last, width + lo : width + lo + HEAD_DIM]
            value = qkv_ref[0:last, 2 * width + lo : 2 * width + lo + HEAD_DIM]
            mixed_grad = do_ref[first:last, lo : lo + HEAD_DIM]
            scores = scores_turned(
                query, key, slope, first, row_ref[:, first:last], col_ref[0:last, :], first
            )
            softmaxed = jnp.exp(scores - lse_ref[head : head + 1, first:last])
            prob_grad = dot(value, mixed_grad, ROWS)
            delta = jnp.sum(softmaxed * prob_grad, axis=0, keepdims=True)
            score_grad = (softmaxed * (prob_grad - delta)).astype(jnp.bfloat16)
            prob_low = softmaxed.astype(jnp.bfloat16)
            query_grad = dot(score_grad, key, COLS) * scale
            grad_ref[first:last, lo : lo + HEAD_DIM] = query_grad.astype(jnp.bfloat16)
            key_grad = dot(score_grad, query, NORMAL)
            value_grad = dot(prob_low, mixed_grad, NORMAL)
            if last == length:
                dk_ref[...] = key_grad
                dv_ref[...] = value_grad
            else:
                dk_ref[0:last, :] += key_grad
                dv_ref[0:last, :] += value_grad
        grad_ref[:, width + lo : width + lo + HEAD_DIM] = (dk_ref[...] * scale).astype(jnp.bfloat16)
        grad_ref[:, 2 * width + lo : 2 * width + lo + HEAD_DIM] = dv_ref[...].astype(jnp.bfloat16)


def attention_specs(seqs, length, groups, heads):
    width = heads * HEAD_DIM
    return (
        pl.BlockSpec(memory_space=pltpu.SMEM),
        pl.BlockSpec((None, 1, length), lambda s, t: (s, 0, 0)),
        pl.BlockSpec((None, length, 1), lambda s, t: (s, 0, 0)),
        pl.BlockSpec((None, length, 3 * width), lambda s, t: (s, 0, t)),
        pl.BlockSpec((None, length, width), lambda s, t: (s, 0, t)),
        pl.BlockSpec((None, None, heads, length), lambda s, t: (s, t, 0, 0)),
    )


def attend(slopes, seg_row, seg_col, qkv, groups, heads):
    seqs, length, _ = qkv.shape
    specs = attention_specs(seqs, length, groups, heads)
    block = math.gcd(length, QUERY_BLOCK)
    return pl.pallas_call(
        functools.partial(attend_kernel, heads, block),
        grid=(seqs, groups),
        in_specs=list(specs[:4]),
        out_specs=[specs[4], specs[5]],
        out_shape=[
            jax.ShapeDtypeStruct((seqs, length, groups * heads * HEAD_DIM), jnp.bfloat16),
            jax.ShapeDtypeStruct((seqs, groups, heads, length), jnp.float32),
        ],
        compiler_params=pltpu.CompilerParams(vmem_limit_bytes=40 * 2**20),
        name="attend",
    )(slopes, seg_row, seg_col, qkv)


def attend_back(slopes, seg_row, seg_col, qkv, mixed_grad, log_total, groups, heads):
    seqs, length, _ = qkv.shape
    specs = attention_specs(seqs, length, groups, heads)
    block = math.gcd(length, QUERY_BLOCK)
    return pl.pallas_call(
        functools.partial(attend_back_kernel, heads, block),
        grid=(seqs, groups),
        in_specs=list(specs),
        out_specs=specs[3],
        out_shape=jax.ShapeDtypeStruct(qkv.shape, jnp.bfloat16),
        scratch_shapes=[
            pltpu.VMEM((length, HEAD_DIM), jnp.float32),
            pltpu.VMEM((length, HEAD_DIM), jnp.float32),
        ],
        compiler_params=pltpu.CompilerParams(vmem_limit_bytes=40 * 2**20),
        name="attend_back",
    )(slopes, seg_row, seg_col, qkv, mixed_grad, log_total)


def whole_sequences(
    tokens,
    segment_ids,
    norm1_gain,
    norm1_shift,
    w_query,
    w_key,
    w_value,
    query_bias,
    value_bias,
    w_out,
    out_bias,
    norm2_gain,
    norm2_shift,
    w_up,
    up_bias,
    w_down,
    down_bias,
    out_grad,
):
    dps, ctxs, groups = (lax.axis_size(name) for name in ALL)
    owners = dps * ctxs
    place = lax.axis_index("tensor")
    seqs_local, span, model = tokens.shape
    per_group = seqs_local // groups
    seqs = per_group // ctxs
    length = span * ctxs
    rows = seqs * length
    heads = query_bias.shape[0]
    width = heads * HEAD_DIM
    shard = w_query.shape[0]
    hidden = w_up.shape[1]
    shared = query_bias.shape[1]
    shared_up = up_bias.shape[1]

    def gather(value):
        whole = lax.all_gather(value, ALL, axis=0, tiled=False)
        return whole.reshape((owners, groups) + value.shape)

    def to_sequences(value):
        mine = lax.dynamic_slice_in_dim(value, place * per_group, per_group, axis=0)
        mine = mine.reshape((ctxs, seqs) + value.shape[1:])
        mine = lax.all_to_all(mine, "ctx", split_axis=0, concat_axis=0, tiled=True)
        return jnp.swapaxes(mine, 0, 1)

    def to_spans(value):
        mine = jnp.swapaxes(value.reshape(seqs, ctxs, span, model), 0, 1)
        mine = lax.all_to_all(mine, "ctx", split_axis=0, concat_axis=0, tiled=True)
        mine = mine.reshape(per_group, span, model)
        return lax.all_gather(mine, "tensor", axis=0, tiled=True)

    def by_owner(value, columns):
        return value.reshape(owners, shard, groups, columns).transpose(0, 2, 1, 3)

    def scatter(value):
        return lax.psum_scatter(value, ALL, scatter_dimension=0, tiled=True)

    small = jnp.concatenate(
        [
            norm1_gain,
            norm1_shift,
            out_bias,
            norm2_gain,
            norm2_shift,
            down_bias,
            query_bias.reshape(-1),
            value_bias.reshape(-1),
            up_bias.reshape(-1),
        ]
    )
    first_pack = jnp.concatenate([w_query, w_key, w_value, w_out.T], axis=1)
    pack_width = first_pack.shape[1]
    extra = -(-small.shape[0] // (16 * pack_width)) * 16
    small = jnp.pad(small, (0, extra * pack_width - small.shape[0])).reshape(extra, pack_width)
    first_pack = gather(jnp.concatenate([first_pack, small], axis=0))
    small = first_pack[:, :, shard:].reshape(owners, groups, extra * pack_width)
    first_pack = first_pack[:, :, :shard]
    second_pack = gather(jnp.stack([w_up, w_down.T]))
    vectors = small[:, 0, : 6 * shard].reshape(owners, 6, shard).transpose(1, 0, 2)
    vectors = vectors.reshape(6, model).astype(jnp.float32)
    gain_one, shift_one, bias_out, gain_two, shift_two, bias_down = (
        vectors[index] for index in range(6)
    )

    def heads_bias(first, columns):
        part = small[:, :, first : first + heads * columns]
        part = part.reshape(owners, groups, heads, columns).transpose(1, 2, 0, 3)
        return part.reshape(groups, heads * columns * owners).astype(jnp.float32)

    bias_first = 6 * shard
    bias_query = heads_bias(bias_first, shared)
    bias_value = heads_bias(bias_first + heads * shared, shared)
    bias_up = heads_bias(bias_first + 2 * heads * shared, shared_up).reshape(-1)
    bias_qkv = jnp.stack([bias_query, jnp.zeros_like(bias_query), bias_value], axis=1).reshape(-1)

    full_qkv = first_pack[..., : 3 * width].transpose(0, 2, 1, 3)
    full_qkv = full_qkv.reshape(model, groups * 3 * width)
    turned_out = first_pack[..., 3 * width :].transpose(0, 2, 1, 3).reshape(model, groups * width)
    full_up = second_pack[:, :, 0].transpose(0, 2, 1, 3).reshape(model, groups * hidden)
    turned_down = second_pack[:, :, 1].transpose(0, 2, 1, 3).reshape(model, groups * hidden)

    inputs_low = to_sequences(tokens)
    segs = to_sequences(segment_ids)
    cotangent = to_sequences(out_grad).reshape(rows, model)
    seg_row = segs.reshape(seqs, 1, length)
    seg_col = segs.reshape(seqs, length, 1)
    slopes = jnp.exp2(-8.0 * jnp.arange(1, HEADS + 1).astype(jnp.float32) / HEADS)

    inputs = inputs_low.reshape(rows, model).astype(jnp.float32)
    normed_one = layer_norm(inputs, gain_one, shift_one).astype(jnp.bfloat16)
    qkv = (matmul(normed_one, full_qkv) + bias_qkv).astype(jnp.bfloat16)
    qkv = qkv.reshape(seqs, length, groups * 3 * width)
    mixed, log_total = attend(slopes, seg_row, seg_col, qkv, groups, heads)
    mixed = mixed.reshape(rows, groups * width)
    residual = inputs + matmul_right(mixed, turned_out) + bias_out
    normed_two = layer_norm(residual, gain_two, shift_two).astype(jnp.bfloat16)
    pre_act = matmul(normed_two, full_up) + bias_up
    activated = gelu_tanh(pre_act).astype(jnp.bfloat16)
    result = (residual + matmul_right(activated, turned_down) + bias_down).astype(jnp.bfloat16)
    outputs = to_spans(result.reshape(seqs, length, model))

    act_grad = matmul(cotangent, turned_down)
    unused, gelu_pull = jax.vjp(gelu_tanh, pre_act)
    pre_grad = gelu_pull(act_grad)[0].astype(jnp.bfloat16)
    grad_down = matmul_left(cotangent, activated).astype(jnp.bfloat16)
    grad_ubias = jnp.sum(pre_grad.astype(jnp.float32), axis=0)
    grad_up = matmul_left(normed_two, pre_grad).astype(jnp.bfloat16)
    grad_ff = jnp.stack([by_owner(grad_up, hidden), by_owner(grad_down, hidden)], axis=2)
    grad_ff, outputs = lax.optimization_barrier((grad_ff, outputs))
    sum_ff = scatter(grad_ff.reshape(-1, hidden)).astype(jnp.float32)
    sum_up = sum_ff[:shard]
    sum_down = sum_ff[shard:].T
    normed_two_back = matmul_right(pre_grad, full_up)
    unused, norm_pull = jax.vjp(layer_norm, residual, gain_two, shift_two)
    resid_grad, gain_two_grad, shift_two_grad = norm_pull(normed_two_back)
    cot_rows = cotangent.astype(jnp.float32)
    resid_grad = resid_grad + cot_rows
    attn_grad = resid_grad.astype(jnp.bfloat16)
    mixed_grad = matmul(attn_grad, turned_out).astype(jnp.bfloat16)
    grad_wout = matmul_left(attn_grad, mixed).astype(jnp.bfloat16)
    qkv_grad = attend_back(
        slopes,
        seg_row,
        seg_col,
        qkv,
        mixed_grad.reshape(seqs, length, groups * width),
        log_total,
        groups,
        heads,
    ).reshape(rows, groups * 3 * width)
    normed_one_back = matmul_right(qkv_grad, full_qkv)
    unused, first_pull = jax.vjp(layer_norm, inputs, gain_one, shift_one)
    input_grad, gain_one_grad, shift_one_grad = first_pull(normed_one_back)
    input_grad = (input_grad + resid_grad).astype(jnp.bfloat16)
    tokens_grad = to_spans(input_grad.reshape(seqs, length, model))
    grad_qkv = matmul_left(normed_one, qkv_grad).astype(jnp.bfloat16)
    grad_pack = jnp.concatenate(
        [by_owner(grad_qkv, 3 * width), by_owner(grad_wout, width)], axis=3
    )
    grad_bias = jnp.sum(qkv_grad.astype(jnp.float32), axis=0).reshape(groups, 3, heads, HEAD_DIM)

    grad_vectors = jnp.stack(
        [
            gain_one_grad,
            shift_one_grad,
            jnp.sum(resid_grad, axis=0),
            gain_two_grad,
            shift_two_grad,
            jnp.sum(cot_rows, axis=0),
        ]
    )
    grad_vectors = grad_vectors.reshape(6, owners, shard).transpose(1, 0, 2)
    grad_vectors = jnp.broadcast_to(
        grad_vectors.reshape(owners, 1, 6 * shard), (owners, groups, 6 * shard)
    )

    def owner_bias(value, columns):
        value = value.reshape(groups, heads, owners, columns).transpose(2, 0, 1, 3)
        return value.reshape(owners, groups, heads * columns)

    grad_small = jnp.concatenate(
        [
            grad_vectors,
            owner_bias(grad_bias[:, 0], shared),
            owner_bias(grad_bias[:, 2], shared),
            owner_bias(grad_ubias, shared_up),
        ],
        axis=2,
    )
    grad_small = grad_small.astype(jnp.bfloat16)
    padding = extra * pack_width - grad_small.shape[2]
    grad_small = jnp.pad(grad_small, ((0, 0), (0, 0), (0, padding)))
    grad_small = grad_small.reshape(owners, groups, extra, pack_width)
    grad_pack = jnp.concatenate([grad_pack, grad_small], axis=2)
    sum_pack = scatter(grad_pack.reshape(-1, pack_width)).astype(jnp.float32)
    sum_small = sum_pack[shard:].reshape(-1)
    sum_qkv = sum_pack[:shard, : 3 * width]
    sum_wout = sum_pack[:shard, 3 * width :].T
    sums = sum_small[: 6 * shard].reshape(6, shard)
    sum_biases = sum_small[6 * shard :]
    count = heads * shared
    return (
        outputs,
        tokens_grad,
        sums[0],
        sums[1],
        sum_qkv[:, :width],
        sum_qkv[:, width : 2 * width],
        sum_qkv[:, 2 * width :],
        sum_biases[:count].reshape(heads, shared),
        sum_biases[count : 2 * count].reshape(heads, shared),
        sum_wout,
        sums[2],
        sums[3],
        sums[4],
        sum_up,
        sum_biases[2 * count : 2 * count + heads * shared_up].reshape(heads, shared_up),
        sum_down,
        sums[5],
    )


def choose_plan(tokens, *others):
    if tokens.shape[0] % (lax.axis_size("ctx") * lax.axis_size("tensor")) == 0:
        return whole_sequences(tokens, *others)
    return shards(tokens, *others)


def solution(mesh):
    return jax.shard_map(
        choose_plan,
        mesh=mesh,
        in_specs=(
            P("dp", "ctx", None),
            P("dp", "ctx"),
            P(("dp", "ctx")),
            P(("dp", "ctx")),
            P(("dp", "ctx"), "tensor"),
            P(("dp", "ctx"), "tensor"),
            P(("dp", "ctx"), "tensor"),
            P("tensor", ("dp", "ctx")),
            P("tensor", ("dp", "ctx")),
            P("tensor", ("dp", "ctx")),
            P(("dp", "ctx")),
            P(("dp", "ctx")),
            P(("dp", "ctx")),
            P(("dp", "ctx"), "tensor"),
            P("tensor", ("dp", "ctx")),
            P("tensor", ("dp", "ctx")),
            P(("dp", "ctx")),
            P("dp", "ctx", None),
        ),
        out_specs=(
            P("dp", "ctx", None),
            P("dp", "ctx", None),
            P(("dp", "ctx")),
            P(("dp", "ctx")),
            P(("dp", "ctx"), "tensor"),
            P(("dp", "ctx"), "tensor"),
            P(("dp", "ctx"), "tensor"),
            P("tensor", ("dp", "ctx")),
            P("tensor", ("dp", "ctx")),
            P("tensor", ("dp", "ctx")),
            P(("dp", "ctx")),
            P(("dp", "ctx")),
            P(("dp", "ctx")),
            P(("dp", "ctx"), "tensor"),
            P("tensor", ("dp", "ctx")),
            P("tensor", ("dp", "ctx")),
            P(("dp", "ctx")),
        ),
        check_vma=False,
    )
```
